32 devices in a mesh: robot: 2 (over x), xy: 4 (over z), yz: 4 (over y, core).
Axes of the slice: x: 2, y: 2, z: 4, core: 2. Of those that a mesh axis runs over, the one named last changes fastest.
Arguments:
- seed_cost: bfloat16 [4, 64, 512, 512], P('robot', None, 'xy', 'yz'), may hold values from 0 to 9
- occupied: int32 [64, 512, 512], P(None, 'xy', 'yz'), may hold values from 0 to 1, as said below
- unknown: int32 [64, 512, 512], P(None, 'xy', 'yz'), may hold values from 0 to 1, as said below
Outputs:
- signed: float32 [64, 512, 512], P(('robot', 'xy'), 'yz')
The draws below stay inside these ranges and needn't reach their ends.
Inputs may be any that keep to these rules, and one draw needn't show every extreme that they name: At least one cell is occupied. At least one cell is neither occupied nor unknown.
All inputs are finite; a program needn't handle non-finite values.
Results may differ from the reference program's by a relative error of at most 0.0003.
Values may be sent and summed in bfloat16 or wider, within the bound.
A program may use at most 64 MiB of HBM per device.

```python
import jax
import jax.numpy as jnp
from jax import lax

NX = 512
NY = 512
NZ = 64
ROBOTS = 4


def inside_range(places, low, high):
    return (places >= low) & (places < high)


def box_mask(depth_part, row_part, column_part):
    return depth_part[:, None, None] & row_part[None, :, None] & column_part[None, None, :]


def draw_occupied(key, part):
    base = jax.random.fold_in(key, 7301)
    depth_index = jnp.arange(NZ, dtype=jnp.int32)
    row_index = jnp.arange(NX, dtype=jnp.int32)
    column_index = jnp.arange(NY, dtype=jnp.int32)
    filled = jnp.zeros((NZ, NX, NY), dtype=jnp.bool_)
    for wall_number in range(8):
        sub_keys = jax.random.split(jax.random.fold_in(base, wall_number), 8)
        facing = jax.random.randint(sub_keys[0], (), 0, 2)
        place_row = jax.random.randint(sub_keys[1], (), 0, NX)
        place_column = jax.random.randint(sub_keys[2], (), 0, NY)
        start_row = jax.random.randint(sub_keys[3], (), 0, NX)
        start_column = jax.random.randint(sub_keys[4], (), 0, NY)
        length_row = jax.random.randint(sub_keys[5], (), NX // 8, NX // 2 + 1)
        length_column = jax.random.randint(sub_keys[6], (), NY // 8, NY // 2 + 1)
        height = jax.random.randint(sub_keys[7], (), NZ // 2, NZ + 1)
        rows_part = jnp.where(facing == 0, inside_range(row_index, place_row, place_row + 1), inside_range(row_index, start_row, start_row + length_row))
        columns_part = jnp.where(facing == 0, inside_range(column_index, start_column, start_column + length_column), inside_range(column_index, place_column, place_column + 1))
        depths_part = inside_range(depth_index, 0, height)
        filled = filled | box_mask(depths_part, rows_part, columns_part)
    for object_number in range(3):
        sub_keys = jax.random.split(jax.random.fold_in(base, 100 + object_number), 6)
        low_depth = jax.random.randint(sub_keys[0], (), 0, NZ)
        side_depth = jax.random.randint(sub_keys[1], (), 2, 17)
        low_row = jax.random.randint(sub_keys[2], (), 0, NX)
        side_row = jax.random.randint(sub_keys[3], (), 2, 17)
        low_column = jax.random.randint(sub_keys[4], (), 0, NY)
        side_column = jax.random.randint(sub_keys[5], (), 2, 17)
        filled = filled | box_mask(inside_range(depth_index, low_depth, low_depth + side_depth), inside_range(row_index, low_row, low_row + side_row), inside_range(column_index, low_column, low_column + side_column))
    return filled.astype(jnp.int32)


def draw_unknown(key, part):
    base = jax.random.fold_in(key, 9203)
    depth_index = jnp.arange(NZ, dtype=jnp.int32)
    row_index = jnp.arange(NX, dtype=jnp.int32)
    column_index = jnp.arange(NY, dtype=jnp.int32)
    region = jnp.zeros((NZ, NX, NY), dtype=jnp.bool_)
    for region_number in range(2):
        sub_keys = jax.random.split(jax.random.fold_in(base, region_number), 5)
        low_row = jax.random.randint(sub_keys[0], (), 0, NX)
        side_row = jax.random.randint(sub_keys[1], (), NX // 4, 3 * NX // 4 + 1)
        low_column = jax.random.randint(sub_keys[2], (), 0, NY)
        side_column = jax.random.randint(sub_keys[3], (), NY // 4, 3 * NY // 4 + 1)
        height = jax.random.randint(sub_keys[4], (), NZ // 2, 3 * NZ // 4 + 1)
        region = region | box_mask(inside_range(depth_index, 0, height), inside_range(row_index, low_row, low_row + side_row), inside_range(column_index, low_column, low_column + side_column))
    speckle = jax.random.randint(jax.random.fold_in(base, 50), (NZ, NX, NY), 0, 16) == 0
    return (region | speckle).astype(jnp.int32)


def block_levels(stream_key, shape, shards, low, high):
    def one(axis_at, blocks):
        draws = jax.random.uniform(jax.random.fold_in(jax.random.fold_in(stream_key, 6), axis_at), (blocks,), jnp.float32, low / len(shards), high / len(shards))
        return jnp.repeat(jnp.exp(draws), shape[axis_at] // blocks).reshape((-1,) + (1,) * (len(shape) - axis_at - 1))

    loudness = one(*shards[0])
    for cut in shards[1:]:
        loudness = loudness * one(*cut)
    return loudness


def setup_inputs(seed: int = 0) -> dict:
    key_of = jax.random.split(jax.random.key(seed), 4)
    seed_cost = jnp.clip(9.0 * jax.random.uniform(key_of[0], (ROBOTS, NZ, NX, NY), jnp.float32) ** block_levels(key_of[0], (ROBOTS, NZ, NX, NY), ((0, 2), (2, 4), (3, 4)), -0.2, 0.2), 0.0, 9.0).astype(jnp.bfloat16)
    occupied = draw_occupied(jax.random.fold_in(key_of[3], 71), 0)
    unknown = draw_unknown(jax.random.fold_in(key_of[3], 71), 0)
    return {"seed_cost": seed_cost, "occupied": occupied, "unknown": unknown}


penalty = 1048576.0
voxel_size = 0.2

def lower_envelope(values, along):
    extent = values.shape[along]
    block_size = min(extent, 128)
    places = jnp.arange(extent, dtype=jnp.float32)
    pieces = []
    for offset in range(0, extent, block_size):
        target = places[offset:offset + block_size]
        table = (places[:, None] - target[None, :]) ** 2
        layout = [1] * (values.ndim + 1)
        layout[along] = extent
        layout[along + 1] = block_size
        summed = jnp.expand_dims(values, along + 1) + table.reshape(layout)
        pieces.append(lax.optimization_barrier(jnp.min(summed, axis=along)))
    return jnp.concatenate(pieces, axis=along)

def depth_pass(layer_plane):
    return lower_envelope(layer_plane, 0)

def column_pass(layer_plane):
    return lower_envelope(layer_plane, 1)

def three_passes(field):
    field = jnp.transpose(lax.map(depth_pass, jnp.transpose(field, (1, 0, 2))), (1, 0, 2))
    field = lax.map(depth_pass, field)
    field = lax.map(column_pass, field)
    return field

def reference(seed_cost, occupied, unknown):
    merged = lax.optimization_barrier(jnp.min(seed_cost, axis=0))
    merged_cost = merged.astype(jnp.float32)
    outside = jnp.where(occupied == 1, merged_cost, merged_cost + penalty)
    inside = jnp.where((occupied == 1) | (unknown == 1), merged_cost + penalty, merged_cost)
    far_out = three_passes(outside)
    far_in = three_passes(inside)
    return voxel_size * (jnp.sqrt(far_out) - jnp.sqrt(far_in))
```

```python
import functools
import math

import jax
import jax.numpy as jnp
from jax import lax
from jax.experimental import pallas as pl
from jax.experimental.pallas import tpu as pltpu
from jax.sharding import PartitionSpec as P

penalty = 1048576.0
voxel_size = 0.2
largest_cost = 9.0
sharpness = 20.0
codes = 65535.0
span = math.log(1.0 + sharpness * (penalty + 1024.0))
block = 16
far_away = 4194304.0


def lower_envelope(values, along):
    extent = values.shape[along]
    block_size = min(extent, 128)
    places = jnp.arange(extent, dtype=jnp.float32)
    pieces = []
    for offset in range(0, extent, block_size):
        target = places[offset : offset + block_size]
        table = (places[:, None] - target[None, :]) ** 2
        layout = [1] * (values.ndim + 1)
        layout[along] = extent
        layout[along + 1] = block_size
        summed = jnp.expand_dims(values, along + 1) + table.reshape(layout)
        pieces.append(jnp.min(summed, axis=along))
    return jnp.concatenate(pieces, axis=along)


def seed_fields(lowest_cost, occupied, unknown):
    merged_cost = lowest_cost.astype(jnp.float32)
    outside = jnp.where(occupied == 1, merged_cost, merged_cost + penalty)
    inside = jnp.where((occupied == 1) | (unknown == 1), merged_cost + penalty, merged_cost)
    return jnp.stack([outside, inside])


def plain_body(seed_cost, occupied, unknown):
    local_lowest = jnp.min(seed_cost, axis=0)
    merged = lax.pmin(local_lowest, "robot")
    fields = lower_envelope(seed_fields(merged, occupied, unknown), 1)
    half_depth = fields.shape[1] // lax.axis_size("robot")
    own_half = lax.dynamic_slice_in_dim(fields, lax.axis_index("robot") * half_depth, half_depth, 1)
    crossed = lower_envelope(lax.all_to_all(own_half, "xy", split_axis=1, concat_axis=2, tiled=True), 2)
    settled = lower_envelope(lax.all_to_all(crossed, "yz", split_axis=2, concat_axis=3, tiled=True), 3)
    return voxel_size * (jnp.sqrt(settled[0]) - jnp.sqrt(settled[1]))


def encode(field):
    scaled = jnp.log(1.0 + sharpness * field) * (codes / span) + 0.5
    return (jnp.minimum(scaled, codes).astype(jnp.int32) - 32768).astype(jnp.int16)


def decode(code):
    scaled = (code.astype(jnp.int32) + 32768).astype(jnp.float32)
    return (jnp.exp(scaled * (span / codes)) - 1.0) * (1.0 / sharpness)


def depth_kernel(place_ref, cost_ref, other_ref, occupied_ref, unknown_ref, out_ref, in_ref, g_ref, h_ref):
    depth = other_ref.shape[0]
    rows, lanes = other_ref.shape[1:]
    reach = math.isqrt(int(largest_cost)) + 1
    wall = jnp.full((rows, lanes), far_away, jnp.float32)
    for field in range(2):
        for pad in range(reach):
            g_ref[field, pad] = wall
            g_ref[field, depth + reach + pad] = wall

    def seeds(z, carry):
        merged = jnp.minimum(jnp.minimum(cost_ref[0, z], cost_ref[1, z]), other_ref[z]).astype(jnp.float32)
        occupied = occupied_ref[z] == 1
        blocked = occupied | (unknown_ref[z] == 1)
        fields = (jnp.where(occupied, merged, merged + penalty), jnp.where(blocked, merged + penalty, merged))
        after = []
        for field, (cost, away) in zip(range(2), carry):
            value = fields[field]
            g_ref[field, z + reach] = value
            seed = value < penalty
            cost = jnp.where(seed, value, cost)
            away = jnp.where(seed, 0.0, away + 1.0)
            h_ref[field, z] = cost + away * away
            after.append((cost, away))
        return tuple(after)

    nothing = jnp.zeros((rows, lanes), jnp.float32)
    lax.fori_loop(0, depth, seeds, ((wall, nothing), (wall, nothing)), unroll=4)

    def settle(step, carry):
        z = depth - 1 - step
        after = []
        for field, (cost, away) in zip(range(2), carry):
            value = g_ref[field, z + reach]
            seed = value < penalty
            cost = jnp.where(seed, value, cost)
            away = jnp.where(seed, 0.0, away + 1.0)
            best = jnp.minimum(jnp.minimum(h_ref[field, z], cost + away * away), value)
            for apart in range(1, reach + 1):
                pair = jnp.minimum(g_ref[field, z + reach - apart], g_ref[field, z + reach + apart])
                best = jnp.minimum(best, pair + float(apart * apart))
            (out_ref, in_ref)[field][z] = encode(best)
            after.append((cost, away))
        return tuple(after)

    lax.fori_loop(0, depth, settle, ((wall, nothing), (wall, nothing)), unroll=4)


def depth_pass(seed_cost, other, occupied, unknown, half):
    robots, depth, _, lanes = seed_cost.shape
    rows = 16
    steps = half // rows
    reach = math.isqrt(int(largest_cost)) + 1
    place = (lax.axis_index("robot") * steps).astype(jnp.int32).reshape(1)
    shape = jax.ShapeDtypeStruct((depth, half, lanes), jnp.int16)
    own = pl.BlockSpec((depth, rows, lanes), lambda i, p: (0, p[0] + i, 0))
    here = pl.BlockSpec((depth, rows, lanes), lambda i, p: (0, i, 0))
    return pl.pallas_call(
        depth_kernel,
        out_shape=(shape, shape),
        grid_spec=pltpu.PrefetchScalarGridSpec(
            num_scalar_prefetch=1,
            grid=(steps,),
            in_specs=[pl.BlockSpec((robots, depth, rows, lanes), lambda i, p: (0, 0, p[0] + i, 0)), here, own, own],
            out_specs=(here, here),
            scratch_shapes=[
                pltpu.VMEM((2, depth + 2 * reach, rows, lanes), jnp.float32),
                pltpu.VMEM((2, depth, rows, lanes), jnp.float32),
            ],
        ),
        compiler_params=pltpu.CompilerParams(vmem_limit_bytes=40 * 2**20),
        name="depth_pass",
    )(place, seed_cost, other, occupied, unknown)


def envelope(f_ref, h_ref, low_ref, top_ref, mask_ref, extent, tile):
    blocks = extent // block
    words = -(-blocks // 32)

    def at(i):
        return pl.ds(pl.multiple_of(i * tile, tile), tile)

    def own(b, _):
        g = [f_ref[at(b * block + k), :] for k in range(block)]
        low = functools.reduce(jnp.minimum, g)
        low_ref[b] = low
        top = None
        for i in range(block):
            best = functools.reduce(jnp.minimum, [g[j] + float((i - j) ** 2) for j in range(block)])
            h_ref[at(b * block + i), :] = best
            top = best if top is None else jnp.maximum(top, best)
        top_ref[b] = top
        return 0

    lax.fori_loop(0, blocks, own, 0)

    def bound(b, _):
        gaps = [jnp.abs(b - j) for j in range(blocks)]
        top = top_ref[b]
        for j in range(blocks):
            reach = (gaps[j] * block + (block - 1)).astype(jnp.float32)
            top = jnp.minimum(top, low_ref[j] + reach * reach)
        for word in range(words):
            bits = jnp.zeros(top.shape, jnp.int32)
            for j in range(word * 32, min(blocks, word * 32 + 32)):
                near = ((gaps[j] - 1) * block + 1).astype(jnp.float32)
                value = 1 << (j % 32)
                value = value - 2**32 if value >= 2**31 else value
                bits = bits | jnp.where(low_ref[j] + near * near < top, jnp.int32(value), jnp.int32(0))
            for axis, size in ((0, tile), (1, 128)):
                shift = size // 2
                while shift:
                    bits = bits | pltpu.roll(bits, shift, axis)
                    shift //= 2
            mask_ref[b * words + word] = bits[0, 0]
        return 0

    lax.fori_loop(0, blocks, bound, 0, unroll=4)

    def outer(b, _):
        def inner(j, _):
            wanted = lax.shift_right_logical(mask_ref[b * words + j // 32], j % 32) & 1

            @pl.when((wanted == 1) & (j != b))
            def _():
                apart = jnp.full((tile, 128), ((b - j) * block).astype(jnp.float32))
                square = {}
                for k in range(1 - block, block):
                    gap = apart + float(k)
                    square[k] = gap * gap
                best = [h_ref[at(b * block + i), :] for i in range(block)]
                for k in range(block):
                    g = f_ref[at(j * block + k), :]
                    best = [jnp.minimum(best[i], g + square[i - k]) for i in range(block)]
                for i in range(block):
                    h_ref[at(b * block + i), :] = best[i]

            return 0

        return lax.fori_loop(0, blocks, inner, 0)

    lax.fori_loop(0, blocks, outer, 0)


def row_kernel(in_ref, out_ref, f_ref, h_ref, low_ref, top_ref, mask_ref, *, robots):
    sources, tile, part, _ = in_ref.shape
    groups = sources // robots
    extent = sources * part
    targets, _, wide, _ = out_ref.shape
    for source in range(sources):
        start = ((source % groups) * robots + source // groups) * part

        def load(z, _, source=source, start=start):
            f_ref[pl.ds(start * tile + z, part, stride=tile), :] = decode(in_ref[source, z])
            return 0

        lax.fori_loop(0, tile, load, 0)
    envelope(f_ref, h_ref, low_ref, top_ref, mask_ref, extent, tile)
    for target in range(targets):

        def store(z, _, target=target):
            out_ref[target, z] = encode(h_ref[pl.ds(target * wide * tile + z, wide, stride=tile), :])
            return 0

        lax.fori_loop(0, tile, store, 0)


def column_kernel(in_ref, *refs):
    if len(refs) == 7:
        prior_ref, refs = refs[0], refs[1:]
    else:
        prior_ref = None
    out_ref, f_ref, h_ref, low_ref, top_ref, mask_ref = refs
    sources, tile, _, part = in_ref.shape
    for source in range(sources):

        def load(z, _, source=source):
            f_ref[pl.ds(source * part * tile + z, part, stride=tile), :] = decode(in_ref[source, z]).T
            return 0

        lax.fori_loop(0, tile, load, 0)
    envelope(f_ref, h_ref, low_ref, top_ref, mask_ref, sources * part, tile)
    for source in range(sources):
        lanes = pl.ds(source * part, part)

        def store(z, _, source=source, lanes=lanes):
            root = jnp.sqrt(h_ref[pl.ds(source * part * tile + z, part, stride=tile), :]).T
            if prior_ref is not None:
                root = voxel_size * (prior_ref[z, :, lanes] - root)
            out_ref[z, :, lanes] = root
            return 0

        lax.fori_loop(0, tile, store, 0)


def scratch(extent, tile):
    blocks = extent // block
    return [
        pltpu.VMEM((extent * tile, 128), jnp.float32),
        pltpu.VMEM((extent * tile, 128), jnp.float32),
        pltpu.VMEM((blocks, tile, 128), jnp.float32),
        pltpu.VMEM((blocks, tile, 128), jnp.float32),
        pltpu.SMEM((blocks * -(-blocks // 32),), jnp.int32),
    ]


def whole_call(kernel, shape, extent, tile, name, *operands):
    vmem = pl.BlockSpec(memory_space=pltpu.VMEM)
    return pl.pallas_call(
        kernel,
        out_shape=shape,
        in_specs=[vmem] * len(operands),
        out_specs=vmem,
        scratch_shapes=scratch(extent, tile),
        compiler_params=pltpu.CompilerParams(vmem_limit_bytes=40 * 2**20),
        name=name,
    )(*operands)


def row_pass(received, robots, targets, name):
    sources, tile, part, lanes = received.shape
    extent = sources * part
    shape = jax.ShapeDtypeStruct((targets, tile, extent // targets, lanes), jnp.int16)
    return whole_call(functools.partial(row_kernel, robots=robots), shape, extent, tile, name, received)


def column_pass(received, name, *prior):
    sources, tile, rows, part = received.shape
    shape = jax.ShapeDtypeStruct((tile, rows, sources * part), jnp.float32)
    return whole_call(column_kernel, shape, sources * part, tile, name, received, *prior)


def fast_body(seed_cost, occupied, unknown):
    robots = lax.axis_size("robot")
    groups = lax.axis_size("xy")
    strips = lax.axis_size("yz")
    depth, rows, lanes = occupied.shape
    half = rows // robots
    tile = depth // (robots * groups)
    me = lax.axis_index("robot")
    for_other = jnp.min(lax.dynamic_slice_in_dim(seed_cost, (1 - me) * half, half, 2), axis=0)
    other = lax.ppermute(for_other, "robot", [(0, 1), (1, 0)])
    fields = depth_pass(seed_cost, other, occupied, unknown, half)
    settled = []
    for field, label in zip(fields, ("out", "in")):
        sent = field.reshape(robots * groups, tile, half, lanes)
        received = lax.all_to_all(sent, ("robot", "xy"), split_axis=0, concat_axis=0, tiled=True)
        crossed = row_pass(received, robots, strips, "row_pass_" + label)
        received = lax.all_to_all(crossed, "yz", split_axis=0, concat_axis=0, tiled=True)
        settled = [column_pass(received, "column_pass_" + label, *settled)]
    return settled[0]


def body(seed_cost, occupied, unknown):
    robots, groups, strips = (lax.axis_size(name) for name in ("robot", "xy", "yz"))
    depth, rows, lanes = occupied.shape
    fits = (
        robots == 2
        and seed_cost.shape[0] == 2
        and lanes == 128
        and rows % (16 * robots) == 0
        and depth == 8 * robots * groups
        and rows * groups == 128 * strips
        and (depth - 1) ** 2 + largest_cost < penalty
    )
    return (fast_body if fits else plain_body)(seed_cost, occupied, unknown)


def solution(mesh):
    in_specs = (P("robot", None, "xy", "yz"), P(None, "xy", "yz"), P(None, "xy", "yz"))
    out_specs = P(("robot", "xy"), "yz", None)
    return jax.shard_map(body, mesh=mesh, in_specs=in_specs, out_specs=out_specs, check_vma=False)
```

```python
import functools
import math

import jax
import jax.numpy as jnp
from jax import lax
from jax.experimental import pallas as pl
from jax.experimental.pallas import tpu as pltpu
from jax.sharding import PartitionSpec as P

penalty = 1048576.0
voxel_size = 0.2
largest_cost = 9.0
sharpness = 20.0
codes = 65535.0
span = math.log(1.0 + sharpness * (penalty + 1024.0))
block = 16
margin = 8
far_away = 4194304.0


def lower_envelope(values, along):
    extent = values.shape[along]
    block_size = min(extent, 128)
    places = jnp.arange(extent, dtype=jnp.float32)
    pieces = []
    for offset in range(0, extent, block_size):
        target = places[offset : offset + block_size]
        table = (places[:, None] - target[None, :]) ** 2
        layout = [1] * (values.ndim + 1)
        layout[along] = extent
        layout[along + 1] = block_size
        summed = jnp.expand_dims(values, along + 1) + table.reshape(layout)
        pieces.append(jnp.min(summed, axis=along))
    return jnp.concatenate(pieces, axis=along)


def seed_fields(lowest_cost, occupied, unknown):
    merged_cost = lowest_cost.astype(jnp.float32)
    outside = jnp.where(occupied == 1, merged_cost, merged_cost + penalty)
    inside = jnp.where((occupied == 1) | (unknown == 1), merged_cost + penalty, merged_cost)
    return jnp.stack([outside, inside])


def plain_body(seed_cost, occupied, unknown):
    local_lowest = jnp.min(seed_cost, axis=0)
    merged = lax.pmin(local_lowest, "robot")
    fields = lower_envelope(seed_fields(merged, occupied, unknown), 1)
    half_depth = fields.shape[1] // lax.axis_size("robot")
    own_half = lax.dynamic_slice_in_dim(fields, lax.axis_index("robot") * half_depth, half_depth, 1)
    crossed = lower_envelope(lax.all_to_all(own_half, "xy", split_axis=1, concat_axis=2, tiled=True), 2)
    settled = lower_envelope(lax.all_to_all(crossed, "yz", split_axis=2, concat_axis=3, tiled=True), 3)
    return voxel_size * (jnp.sqrt(settled[0]) - jnp.sqrt(settled[1]))


def encode(field):
    scaled = jnp.log(1.0 + sharpness * field) * (codes / span) + 0.5
    return (jnp.minimum(scaled, codes).astype(jnp.int32) - 32768).astype(jnp.int16)


def decode(code):
    scaled = (code.astype(jnp.int32) + 32768).astype(jnp.float32)
    return (jnp.exp(scaled * (span / codes)) - 1.0) * (1.0 / sharpness)


def depth_kernel(place_ref, cost_ref, other_ref, occupied_ref, unknown_ref, out_ref, in_ref, g_ref, h_ref):
    depth = other_ref.shape[0]
    rows, lanes = other_ref.shape[1:]
    reach = math.isqrt(int(largest_cost)) + 1
    wall = jnp.full((rows, lanes), far_away, jnp.float32)
    for field in range(2):
        for pad in range(reach):
            g_ref[field, pad] = wall
            g_ref[field, depth + reach + pad] = wall

    def seeds(z, carry):
        merged = jnp.minimum(jnp.minimum(cost_ref[0, z], cost_ref[1, z]), other_ref[z]).astype(jnp.float32)
        occupied = occupied_ref[z] == 1
        blocked = occupied | (unknown_ref[z] == 1)
        fields = (jnp.where(occupied, merged, merged + penalty), jnp.where(blocked, merged + penalty, merged))
        after = []
        for field, (cost, away) in zip(range(2), carry):
            value = fields[field]
            g_ref[field, z + reach] = value
            seed = value < penalty
            cost = jnp.where(seed, value, cost)
            away = jnp.where(seed, 0.0, away + 1.0)
            h_ref[field, z] = cost + away * away
            after.append((cost, away))
        return tuple(after)

    nothing = jnp.zeros((rows, lanes), jnp.float32)
    lax.fori_loop(0, depth, seeds, ((wall, nothing), (wall, nothing)), unroll=4)

    def settle(step, carry):
        z = depth - 1 - step
        after = []
        for field, (cost, away) in zip(range(2), carry):
            value = g_ref[field, z + reach]
            seed = value < penalty
            cost = jnp.where(seed, value, cost)
            away = jnp.where(seed, 0.0, away + 1.0)
            best = jnp.minimum(jnp.minimum(h_ref[field, z], cost + away * away), value)
            for apart in range(1, reach + 1):
                pair = jnp.minimum(g_ref[field, z + reach - apart], g_ref[field, z + reach + apart])
                best = jnp.minimum(best, pair + float(apart * apart))
            (out_ref, in_ref)[field][z] = encode(best)
            after.append((cost, away))
        return tuple(after)

    lax.fori_loop(0, depth, settle, ((wall, nothing), (wall, nothing)), unroll=4)


def depth_pass(seed_cost, other, occupied, unknown, half):
    robots, depth, _, lanes = seed_cost.shape
    rows = 16
    steps = half // rows
    reach = math.isqrt(int(largest_cost)) + 1
    place = (lax.axis_index("robot") * steps).astype(jnp.int32).reshape(1)
    shape = jax.ShapeDtypeStruct((depth, half, lanes), jnp.int16)
    own = pl.BlockSpec((depth, rows, lanes), lambda i, p: (0, p[0] + i, 0))
    here = pl.BlockSpec((depth, rows, lanes), lambda i, p: (0, i, 0))
    return pl.pallas_call(
        depth_kernel,
        out_shape=(shape, shape),
        grid_spec=pltpu.PrefetchScalarGridSpec(
            num_scalar_prefetch=1,
            grid=(steps,),
            in_specs=[pl.BlockSpec((robots, depth, rows, lanes), lambda i, p: (0, 0, p[0] + i, 0)), here, own, own],
            out_specs=(here, here),
            scratch_shapes=[
                pltpu.VMEM((2, depth + 2 * reach, rows, lanes), jnp.float32),
                pltpu.VMEM((2, depth, rows, lanes), jnp.float32),
            ],
        ),
        compiler_params=pltpu.CompilerParams(vmem_limit_bytes=56 * 2**20),
        name="depth_pass",
    )(place, seed_cost, other, occupied, unknown)


def envelope(f_ref, h_ref, low_ref, top_ref, bits_ref, reach_ref, near_ref, list_ref, extent, tile):
    blocks = extent // block
    words = -(-blocks // 32)

    def source(j):
        return pl.ds(pl.multiple_of((margin + j) * tile, tile), tile)

    def target(i):
        return pl.ds(pl.multiple_of(i * tile, tile), tile)

    for pad in range(margin):
        for place in (pad, margin + extent + pad):
            f_ref[place * tile : (place + 1) * tile, :] = jnp.full((tile, 128), far_away, jnp.float32)
    for gap in range(blocks):
        reach = float((gap * block + block - 1) ** 2)
        near = float((gap - 1) * block + 1) ** 2 if gap > 1 else float((margin + 1) ** 2) if gap else 2 * far_away
        for index in {blocks - gap, blocks + gap}:
            reach_ref[index] = jnp.full((tile, 128), reach, jnp.float32)
            near_ref[index] = jnp.full((tile, 128), near, jnp.float32)

    def own(b, _):
        g = [f_ref[source(b * block + k - margin), :] for k in range(block + 2 * margin)]
        low_ref[b] = functools.reduce(jnp.minimum, g[margin : margin + block])
        top = None
        for i in range(block):
            best = g[margin + i]
            for j in range(block + 2 * margin):
                apart = abs(j - margin - i)
                if apart and (apart <= margin or 0 <= j - margin < block):
                    best = jnp.minimum(best, g[j] + float(apart**2))
            h_ref[target(b * block + i), :] = best
            top = best if top is None else jnp.maximum(top, best)
        top_ref[b] = top
        return 0

    lax.fori_loop(0, blocks, own, 0)

    def bound(group, count):
        for r in range(8):
            b = group * 8 + r
            top = top_ref[b]
            for j in range(blocks):
                top = jnp.minimum(top, low_ref[j] + reach_ref[blocks + b - j])
            for word in range(words):
                bits = jnp.zeros(top.shape, jnp.int32)
                for j in range(word * 32, min(blocks, word * 32 + 32)):
                    value = 1 << (j % 32)
                    value = value - 2**32 if value >= 2**31 else value
                    bits = bits | jnp.where(low_ref[j] + near_ref[blocks + b - j] < top, jnp.int32(value), jnp.int32(0))
                bits_ref[word, pl.ds(r * tile, tile), :] = bits
        for word in range(words):
            joined = functools.reduce(jnp.bitwise_or, [bits_ref[word, pl.ds(k, 8, stride=tile), :] for k in range(tile)])
            shift = 64
            while shift:
                joined = joined | pltpu.roll(joined, shift, 1)
                shift //= 2
            for r in range(8):
                mask = joined[r, 0]
                for j in range(word * 32, min(blocks, word * 32 + 32)):
                    list_ref[count] = (group * 8 + r) * 1024 + j
                    count = count + (lax.shift_right_logical(mask, j % 32) & 1)
        return count

    count = lax.fori_loop(0, blocks // 8, bound, jnp.int32(0))

    def visit(k, _):
        code = list_ref[k]
        b = lax.shift_right_logical(code, 10)
        j = code & 1023
        apart = jnp.full((tile, 128), ((b - j) * block).astype(jnp.float32))
        square = {}
        for step in range(1 - block, block):
            gap = apart + float(step)
            square[step] = gap * gap
        best = [h_ref[target(b * block + i), :] for i in range(block)]
        for step in range(block):
            g = f_ref[source(j * block + step), :]
            best = [jnp.minimum(best[i], g + square[i - step]) for i in range(block)]
        for i in range(block):
            h_ref[target(b * block + i), :] = best[i]
        return 0

    lax.fori_loop(0, count, visit, 0)


def row_kernel(in_ref, out_ref, f_ref, h_ref, *rest, robots):
    sources, tile, part, _ = in_ref.shape
    groups = sources // robots
    extent = sources * part
    targets, _, wide, _ = out_ref.shape

    def load(source, _):
        start = (margin + (lax.rem(source, groups) * robots + source // groups) * part) * tile
        for z in range(tile):
            f_ref[pl.ds(start + z, part, stride=tile), :] = decode(in_ref[source, z])
        return 0

    lax.fori_loop(0, sources, load, 0)
    envelope(f_ref, h_ref, *rest, extent, tile)

    def store(target, _):
        for z in range(tile):
            out_ref[target, z] = encode(h_ref[pl.ds(target * wide * tile + z, wide, stride=tile), :])
        return 0

    lax.fori_loop(0, targets, store, 0)


def column_kernel(in_ref, *refs, has_prior):
    prior_ref, refs = (refs[0], refs[1:]) if has_prior else (None, refs)
    out_ref, f_ref, h_ref, *rest = refs
    sources, tile, _, part = in_ref.shape

    def load(z, _):
        for source in range(sources):
            start = (margin + source * part) * tile
            f_ref[pl.ds(start + z, part, stride=tile), :] = decode(in_ref[source, z]).T
        return 0

    lax.fori_loop(0, tile, load, 0)
    envelope(f_ref, h_ref, *rest, sources * part, tile)

    def store(z, _):
        for source in range(sources):
            lanes = pl.ds(source * part, part)
            root = jnp.sqrt(h_ref[pl.ds(source * part * tile + z, part, stride=tile), :]).T
            if has_prior:
                root = voxel_size * (prior_ref[z, :, lanes] - root)
            out_ref[z, :, lanes] = root
        return 0

    lax.fori_loop(0, tile, store, 0)


def scratch(extent, tile):
    blocks = extent // block
    words = -(-blocks // 32)
    return [
        pltpu.VMEM(((extent + 2 * margin) * tile, 128), jnp.float32),
        pltpu.VMEM((extent * tile, 128), jnp.float32),
        pltpu.VMEM((blocks, tile, 128), jnp.float32),
        pltpu.VMEM((blocks, tile, 128), jnp.float32),
        pltpu.VMEM((words, 8 * tile, 128), jnp.int32),
        pltpu.VMEM((2 * blocks, tile, 128), jnp.float32),
        pltpu.VMEM((2 * blocks, tile, 128), jnp.float32),
        pltpu.SMEM((blocks * blocks + 1,), jnp.int32),
    ]


def whole_call(kernel, shape, extent, tile, name, *operands):
    vmem = pl.BlockSpec(memory_space=pltpu.VMEM)
    return pl.pallas_call(
        kernel,
        out_shape=shape,
        in_specs=[vmem] * len(operands),
        out_specs=vmem,
        scratch_shapes=scratch(extent, tile),
        compiler_params=pltpu.CompilerParams(vmem_limit_bytes=56 * 2**20),
        name=name,
    )(*operands)


def row_pass(received, robots, targets, name):
    sources, tile, part, lanes = received.shape
    extent = sources * part
    shape = jax.ShapeDtypeStruct((targets, tile, extent // targets, lanes), jnp.int16)
    return whole_call(functools.partial(row_kernel, robots=robots), shape, extent, tile, name, received)


def column_pass(received, name, *prior):
    sources, tile, rows, part = received.shape
    shape = jax.ShapeDtypeStruct((tile, rows, sources * part), jnp.float32)
    return whole_call(functools.partial(column_kernel, has_prior=bool(prior)), shape, sources * part, tile, name, received, *prior)


def fast_body(seed_cost, occupied, unknown):
    robots = lax.axis_size("robot")
    groups = lax.axis_size("xy")
    strips = lax.axis_size("yz")
    depth, rows, lanes = occupied.shape
    half = rows // robots
    tile = depth // (robots * groups)
    me = lax.axis_index("robot")
    for_other = jnp.min(lax.dynamic_slice_in_dim(seed_cost, (1 - me) * half, half, 2), axis=0)
    other = lax.ppermute(for_other, "robot", [(0, 1), (1, 0)])
    fields = depth_pass(seed_cost, other, occupied, unknown, half)
    settled = []
    for field, label in zip(fields, ("out", "in")):
        sent = field.reshape(robots * groups, tile, half, lanes)
        received = lax.all_to_all(sent, ("robot", "xy"), split_axis=0, concat_axis=0, tiled=True)
        crossed = row_pass(received, robots, strips, "row_pass_" + label)
        received = lax.all_to_all(crossed, "yz", split_axis=0, concat_axis=0, tiled=True)
        settled = [column_pass(received, "column_pass_" + label, *settled)]
    return settled[0]


def body(seed_cost, occupied, unknown):
    robots, groups, strips = (lax.axis_size(name) for name in ("robot", "xy", "yz"))
    depth, rows, lanes = occupied.shape
    fits = (
        robots == 2
        and seed_cost.shape[0] == 2
        and lanes == 128
        and rows % (16 * robots) == 0
        and depth == 8 * robots * groups
        and rows * groups == 128 * strips
        and rows * groups % (8 * block) == 0
        and (depth - 1) ** 2 + largest_cost < penalty
    )
    return (fast_body if fits else plain_body)(seed_cost, occupied, unknown)


def solution(mesh):
    in_specs = (P("robot", None, "xy", "yz"), P(None, "xy", "yz"), P(None, "xy", "yz"))
    out_specs = P(("robot", "xy"), "yz", None)
    return jax.shard_map(body, mesh=mesh, in_specs=in_specs, out_specs=out_specs, check_vma=False)
```

```python
import functools
import math

import jax
import jax.numpy as jnp
from jax import lax
from jax.experimental import pallas as pl
from jax.experimental.pallas import tpu as pltpu
from jax.sharding import PartitionSpec as P

penalty = 1048576.0
voxel_size = 0.2
largest_cost = 9.0
sharpness = 20.0
codes = 65535.0
span = math.log(1.0 + sharpness * (penalty + 1024.0))
block = 16
margin = 8
far_away = 4194304.0


def lower_envelope(values, along):
    extent = values.shape[along]
    block_size = min(extent, 128)
    places = jnp.arange(extent, dtype=jnp.float32)
    pieces = []
    for offset in range(0, extent, block_size):
        target = places[offset : offset + block_size]
        table = (places[:, None] - target[None, :]) ** 2
        layout = [1] * (values.ndim + 1)
        layout[along] = extent
        layout[along + 1] = block_size
        summed = jnp.expand_dims(values, along + 1) + table.reshape(layout)
        pieces.append(jnp.min(summed, axis=along))
    return jnp.concatenate(pieces, axis=along)


def seed_fields(lowest_cost, occupied, unknown):
    merged_cost = lowest_cost.astype(jnp.float32)
    outside = jnp.where(occupied == 1, merged_cost, merged_cost + penalty)
    inside = jnp.where((occupied == 1) | (unknown == 1), merged_cost + penalty, merged_cost)
    return jnp.stack([outside, inside])


def plain_body(seed_cost, occupied, unknown):
    local_lowest = jnp.min(seed_cost, axis=0)
    merged = lax.pmin(local_lowest, "robot")
    fields = lower_envelope(seed_fields(merged, occupied, unknown), 1)
    half_depth = fields.shape[1] // lax.axis_size("robot")
    own_half = lax.dynamic_slice_in_dim(fields, lax.axis_index("robot") * half_depth, half_depth, 1)
    crossed = lower_envelope(lax.all_to_all(own_half, "xy", split_axis=1, concat_axis=2, tiled=True), 2)
    settled = lower_envelope(lax.all_to_all(crossed, "yz", split_axis=2, concat_axis=3, tiled=True), 3)
    return voxel_size * (jnp.sqrt(settled[0]) - jnp.sqrt(settled[1]))


def encode(field):
    scaled = jnp.log(1.0 + sharpness * field) * (codes / span) + 0.5
    return (jnp.minimum(scaled, codes).astype(jnp.int32) - 32768).astype(jnp.int16)


def decode(code):
    scaled = (code.astype(jnp.int32) + 32768).astype(jnp.float32)
    return (jnp.exp(scaled * (span / codes)) - 1.0) * (1.0 / sharpness)


def depth_kernel(
    cost_ref, occupied_ref, unknown_ref, out_ref, in_ref,
    cost_other, cost_own, occupied_own, unknown_own, gone, come, code, g_ref, h_ref,
    other_sem, own_sem, gone_sem, come_sem, send_sem, recv_sem, keep_sem,
):
    robots, groups = lax.axis_size("robot"), lax.axis_size("xy")
    robot, group = lax.axis_index("robot"), lax.axis_index("xy")
    members = robots * groups
    me = robot * groups + group
    chunks, depth, rows, lanes = gone.shape
    half = chunks * rows
    tile = depth // members
    reach = math.isqrt(int(largest_cost)) + 1

    def place(member):
        return {"robot": member // groups, "xy": lax.rem(member, groups)}

    def span_of(owner, c):
        return pl.ds(pl.multiple_of(owner * half + c * rows, rows), rows)

    def fetch_other(c):
        return pltpu.make_async_copy(cost_ref.at[:, :, span_of(1 - robot, c), :], cost_other.at[c], other_sem.at[c])

    def fetch_own(c):
        return (
            pltpu.make_async_copy(cost_ref.at[:, :, span_of(robot, c), :], cost_own.at[c], own_sem.at[0, c]),
            pltpu.make_async_copy(occupied_ref.at[:, span_of(robot, c), :], occupied_own.at[c], own_sem.at[1, c]),
            pltpu.make_async_copy(unknown_ref.at[:, span_of(robot, c), :], unknown_own.at[c], own_sem.at[2, c]),
        )

    def hand_over(c):
        return pltpu.make_async_remote_copy(
            src_ref=gone.at[c], dst_ref=come.at[c], send_sem=gone_sem.at[c], recv_sem=come_sem.at[c],
            device_id={"robot": 1 - robot}, device_id_type=pl.DeviceIdType.MESH,
        )

    def send(c, step):
        member = lax.rem(me + step, members)
        return pltpu.make_async_remote_copy(
            src_ref=code.at[0, c, pl.ds(member * tile, tile)], dst_ref=out_ref.at[me, :, span_of(0, c), :],
            send_sem=send_sem.at[c, step - 1], recv_sem=recv_sem.at[c, step - 1],
            device_id=place(member), device_id_type=pl.DeviceIdType.MESH,
        )

    def keep(c):
        return (
            pltpu.make_async_copy(code.at[0, c, pl.ds(me * tile, tile)], out_ref.at[me, :, span_of(0, c), :], keep_sem.at[0, c]),
            pltpu.make_async_copy(code.at[1, c], in_ref.at[:, span_of(0, c), :], keep_sem.at[1, c]),
        )

    def over_chunks(do):
        def step(c, _):
            do(c)
            return 0

        lax.fori_loop(0, chunks, step, 0)

    def begin(c):
        fetch_other(c).start()

    over_chunks(begin)

    def begin_own(c):
        for copy in fetch_own(c):
            copy.start()

    over_chunks(begin_own)

    barrier = pltpu.get_barrier_semaphore()
    for step in range(1, members):
        pl.semaphore_signal(barrier, inc=1, device_id=place(lax.rem(me + step, members)), device_id_type=pl.DeviceIdType.MESH)
    pl.semaphore_wait(barrier, members - 1)

    def merge(c):
        fetch_other(c).wait()
        gone[c] = jnp.minimum(cost_other[c, 0], cost_other[c, 1])
        hand_over(c).start()

    over_chunks(merge)

    wall = jnp.full((rows, lanes), far_away, jnp.float32)
    nothing = jnp.zeros((rows, lanes), jnp.float32)
    for field in range(2):
        for pad in range(reach):
            g_ref[field, pad] = wall
            g_ref[field, depth + reach + pad] = wall

    def pass_chunk(c):
        for copy in fetch_own(c):
            copy.wait()
        hand_over(c).wait_recv()

        def seeds(z, carry):
            merged = jnp.minimum(jnp.minimum(cost_own[c, 0, z], cost_own[c, 1, z]), come[c, z]).astype(jnp.float32)
            occupied = occupied_own[c, z] == 1
            blocked = occupied | (unknown_own[c, z] == 1)
            fields = (jnp.where(occupied, merged, merged + penalty), jnp.where(blocked, merged + penalty, merged))
            after = []
            for field, (cost, away) in zip(range(2), carry):
                value = fields[field]
                g_ref[field, z + reach] = value
                seed = value < penalty
                cost = jnp.where(seed, value, cost)
                away = jnp.where(seed, 0.0, away + 1.0)
                h_ref[field, z] = cost + away * away
                after.append((cost, away))
            return tuple(after)

        lax.fori_loop(0, depth, seeds, ((wall, nothing), (wall, nothing)), unroll=4)

        def settle(step, carry):
            z = depth - 1 - step
            after = []
            for field, (cost, away) in zip(range(2), carry):
                value = g_ref[field, z + reach]
                seed = value < penalty
                cost = jnp.where(seed, value, cost)
                away = jnp.where(seed, 0.0, away + 1.0)
                best = jnp.minimum(jnp.minimum(h_ref[field, z], cost + away * away), value)
                for apart in range(1, reach + 1):
                    pair = jnp.minimum(g_ref[field, z + reach - apart], g_ref[field, z + reach + apart])
                    best = jnp.minimum(best, pair + float(apart * apart))
                code[field, c, z] = encode(best)
                after.append((cost, away))
            return tuple(after)

        lax.fori_loop(0, depth, settle, ((wall, nothing), (wall, nothing)), unroll=4)
        for step in range(1, members):
            send(c, step).start()
        for copy in keep(c):
            copy.start()

    over_chunks(pass_chunk)

    def finish(c):
        hand_over(c).wait_send()
        for copy in keep(c):
            copy.wait()
        for step in range(1, members):
            send(c, step).wait()

    over_chunks(finish)


def depth_pass(seed_cost, occupied, unknown, half, members):
    robots, depth, _, lanes = seed_cost.shape
    rows = 16
    chunks = half // rows
    reach = math.isqrt(int(largest_cost)) + 1
    anywhere = pl.BlockSpec(memory_space=pl.ANY)
    copies = pltpu.SemaphoreType.DMA
    return pl.pallas_call(
        depth_kernel,
        out_shape=(
            jax.ShapeDtypeStruct((members, depth // members, half, lanes), jnp.int16),
            jax.ShapeDtypeStruct((depth, half, lanes), jnp.int16),
        ),
        in_specs=[anywhere] * 3,
        out_specs=(anywhere, anywhere),
        scratch_shapes=[
            pltpu.VMEM((chunks, robots, depth, rows, lanes), jnp.bfloat16),
            pltpu.VMEM((chunks, robots, depth, rows, lanes), jnp.bfloat16),
            pltpu.VMEM((chunks, depth, rows, lanes), jnp.int32),
            pltpu.VMEM((chunks, depth, rows, lanes), jnp.int32),
            pltpu.VMEM((chunks, depth, rows, lanes), jnp.bfloat16),
            pltpu.VMEM((chunks, depth, rows, lanes), jnp.bfloat16),
            pltpu.VMEM((2, chunks, depth, rows, lanes), jnp.int16),
            pltpu.VMEM((2, depth + 2 * reach, rows, lanes), jnp.float32),
            pltpu.VMEM((2, depth, rows, lanes), jnp.float32),
            copies((chunks,)),
            copies((3, chunks)),
            copies((chunks,)),
            copies((chunks,)),
            copies((chunks, members - 1)),
            copies((chunks, members - 1)),
            copies((2, chunks)),
        ],
        compiler_params=pltpu.CompilerParams(vmem_limit_bytes=56 * 2**20, collective_id=0, has_side_effects=True),
        name="depth_pass",
    )(seed_cost, occupied, unknown)


def envelope(f_ref, h_ref, low_ref, top_ref, bits_ref, reach_ref, near_ref, list_ref, extent, tile):
    blocks = extent // block
    words = -(-blocks // 32)

    def source(j):
        return pl.ds(pl.multiple_of((margin + j) * tile, tile), tile)

    def target(i):
        return pl.ds(pl.multiple_of(i * tile, tile), tile)

    for pad in range(margin):
        for place in (pad, margin + extent + pad):
            f_ref[place * tile : (place + 1) * tile, :] = jnp.full((tile, 128), far_away, jnp.float32)
    for gap in range(blocks):
        reach = float((gap * block + block - 1) ** 2)
        near = float((gap - 1) * block + 1) ** 2 if gap > 1 else float((margin + 1) ** 2) if gap else 2 * far_away
        for index in {blocks - gap, blocks + gap}:
            reach_ref[index] = jnp.full((tile, 128), reach, jnp.float32)
            near_ref[index] = jnp.full((tile, 128), near, jnp.float32)

    def own(b, _):
        g = [f_ref[source(b * block + k - margin), :] for k in range(block + 2 * margin)]
        low_ref[b] = functools.reduce(jnp.minimum, g[margin : margin + block])
        top = None
        for i in range(block):
            best = g[margin + i]
            for j in range(block + 2 * margin):
                apart = abs(j - margin - i)
                if apart and (apart <= margin or 0 <= j - margin < block):
                    best = jnp.minimum(best, g[j] + float(apart**2))
            h_ref[target(b * block + i), :] = best
            top = best if top is None else jnp.maximum(top, best)
        top_ref[b] = top
        return 0

    lax.fori_loop(0, blocks, own, 0)

    def bound(group, count):
        for r in range(8):
            b = group * 8 + r
            top = top_ref[b]
            for j in range(blocks):
                top = jnp.minimum(top, low_ref[j] + reach_ref[blocks + b - j])
            for word in range(words):
                bits = jnp.zeros(top.shape, jnp.int32)
                for j in range(word * 32, min(blocks, word * 32 + 32)):
                    value = 1 << (j % 32)
                    value = value - 2**32 if value >= 2**31 else value
                    bits = bits | jnp.where(low_ref[j] + near_ref[blocks + b - j] < top, jnp.int32(value), jnp.int32(0))
                bits_ref[word, pl.ds(r * tile, tile), :] = bits
        for word in range(words):
            joined = functools.reduce(jnp.bitwise_or, [bits_ref[word, pl.ds(k, 8, stride=tile), :] for k in range(tile)])
            shift = 64
            while shift:
                joined = joined | pltpu.roll(joined, shift, 1)
                shift //= 2
            for r in range(8):
                mask = joined[r, 0]
                for first in range(word * 32, min(blocks, word * 32 + 32), 8):
                    some = lax.shift_right_logical(mask, first % 32) & 255

                    def enlist(count, some=some, first=first, b=group * 8 + r):
                        for j in range(8):
                            list_ref[count] = b * 1024 + (first + j)
                            count = count + (lax.shift_right_logical(some, j) & 1)
                        return count

                    count = lax.cond(some != 0, enlist, lambda count: count, count)
        return count

    count = lax.fori_loop(0, blocks // 8, bound, jnp.int32(0))

    def visit(k, _):
        code = list_ref[k]
        b = lax.shift_right_logical(code, 10)
        j = code & 1023
        apart = jnp.full((tile, 128), ((b - j) * block).astype(jnp.float32))
        square = {}
        for step in range(1 - block, block):
            gap = apart + float(step)
            square[step] = gap * gap
        best = [h_ref[target(b * block + i), :] for i in range(block)]
        for step in range(block):
            g = f_ref[source(j * block + step), :]
            best = [jnp.minimum(best[i], g + square[i - step]) for i in range(block)]
        for i in range(block):
            h_ref[target(b * block + i), :] = best[i]
        return 0

    lax.fori_loop(0, count, visit, 0)


def row_kernel(in_ref, out_ref, f_ref, h_ref, *rest, robots):
    sources, tile, part, _ = in_ref.shape
    groups = sources // robots
    extent = sources * part
    targets, _, wide, _ = out_ref.shape

    def load(source, _):
        start = (margin + (lax.rem(source, groups) * robots + source // groups) * part) * tile
        for z in range(tile):
            f_ref[pl.ds(start + z, part, stride=tile), :] = decode(in_ref[source, z])
        return 0

    lax.fori_loop(0, sources, load, 0)
    envelope(f_ref, h_ref, *rest, extent, tile)

    def store(target, _):
        for z in range(tile):
            out_ref[target, z] = encode(h_ref[pl.ds(target * wide * tile + z, wide, stride=tile), :])
        return 0

    lax.fori_loop(0, targets, store, 0)


def column_kernel(in_ref, *refs, has_prior):
    prior_ref, refs = (refs[0], refs[1:]) if has_prior else (None, refs)
    out_ref, f_ref, h_ref, *rest = refs
    sources, tile, _, part = in_ref.shape

    def load(z, _):
        for source in range(sources):
            start = (margin + source * part) * tile
            f_ref[pl.ds(start + z, part, stride=tile), :] = decode(in_ref[source, z]).T
        return 0

    lax.fori_loop(0, tile, load, 0)
    envelope(f_ref, h_ref, *rest, sources * part, tile)

    def store(z, _):
        for source in range(sources):
            lanes = pl.ds(source * part, part)
            root = jnp.sqrt(h_ref[pl.ds(source * part * tile + z, part, stride=tile), :]).T
            if has_prior:
                root = voxel_size * (prior_ref[z, :, lanes] - root)
            out_ref[z, :, lanes] = root
        return 0

    lax.fori_loop(0, tile, store, 0)


def scratch(extent, tile):
    blocks = extent // block
    words = -(-blocks // 32)
    return [
        pltpu.VMEM(((extent + 2 * margin) * tile, 128), jnp.float32),
        pltpu.VMEM((extent * tile, 128), jnp.float32),
        pltpu.VMEM((blocks, tile, 128), jnp.float32),
        pltpu.VMEM((blocks, tile, 128), jnp.float32),
        pltpu.VMEM((words, 8 * tile, 128), jnp.int32),
        pltpu.VMEM((2 * blocks, tile, 128), jnp.float32),
        pltpu.VMEM((2 * blocks, tile, 128), jnp.float32),
        pltpu.SMEM((blocks * blocks + 1,), jnp.int32),
    ]


def whole_call(kernel, shape, extent, tile, name, *operands):
    vmem = pl.BlockSpec(memory_space=pltpu.VMEM)
    return pl.pallas_call(
        kernel,
        out_shape=shape,
        in_specs=[vmem] * len(operands),
        out_specs=vmem,
        scratch_shapes=scratch(extent, tile),
        compiler_params=pltpu.CompilerParams(vmem_limit_bytes=56 * 2**20),
        name=name,
    )(*operands)


def row_pass(received, robots, targets, name):
    sources, tile, part, lanes = received.shape
    extent = sources * part
    shape = jax.ShapeDtypeStruct((targets, tile, extent // targets, lanes), jnp.int16)
    return whole_call(functools.partial(row_kernel, robots=robots), shape, extent, tile, name, received)


def column_pass(received, name, *prior):
    sources, tile, rows, part = received.shape
    shape = jax.ShapeDtypeStruct((tile, rows, sources * part), jnp.float32)
    return whole_call(functools.partial(column_kernel, has_prior=bool(prior)), shape, sources * part, tile, name, received, *prior)


def fast_body(seed_cost, occupied, unknown):
    robots = lax.axis_size("robot")
    groups = lax.axis_size("xy")
    strips = lax.axis_size("yz")
    depth, rows, lanes = occupied.shape
    half = rows // robots
    tile = depth // (robots * groups)
    members = robots * groups
    out_received, in_codes = depth_pass(seed_cost, occupied, unknown, half, members)
    in_received = lax.all_to_all(
        in_codes.reshape(members, tile, half, lanes), ("robot", "xy"), split_axis=0, concat_axis=0, tiled=True
    )
    settled = []
    for received, label in ((out_received, "out"), (in_received, "in")):
        crossed = row_pass(received, robots, strips, "row_pass_" + label)
        received = lax.all_to_all(crossed, "yz", split_axis=0, concat_axis=0, tiled=True)
        settled = [column_pass(received, "column_pass_" + label, *settled)]
    return settled[0]


def body(seed_cost, occupied, unknown):
    robots, groups, strips = (lax.axis_size(name) for name in ("robot", "xy", "yz"))
    depth, rows, lanes = occupied.shape
    fits = (
        robots == 2
        and seed_cost.shape[0] == 2
        and lanes == 128
        and rows % (16 * robots) == 0
        and depth == 8 * robots * groups
        and rows * groups == 128 * strips
        and rows * groups % (8 * block) == 0
        and (depth - 1) ** 2 + largest_cost < penalty
    )
    return (fast_body if fits else plain_body)(seed_cost, occupied, unknown)


def solution(mesh):
    in_specs = (P("robot", None, "xy", "yz"), P(None, "xy", "yz"), P(None, "xy", "yz"))
    out_specs = P(("robot", "xy"), "yz", None)
    return jax.shard_map(body, mesh=mesh, in_specs=in_specs, out_specs=out_specs, check_vma=False)
```

```python
import functools
import math

import jax
import jax.numpy as jnp
from jax import lax
from jax.experimental import pallas as pl
from jax.experimental.pallas import tpu as pltpu
from jax.sharding import PartitionSpec as P

penalty = 1048576.0
voxel_size = 0.2
largest_cost = 9.0
sharpness = 20.0
codes = 65535.0
span = math.log(1.0 + sharpness * (penalty + 1024.0))
block = 16
margin = 8
far_away = 4194304.0


def lower_envelope(values, along):
    extent = values.shape[along]
    block_size = min(extent, 128)
    places = jnp.arange(extent, dtype=jnp.float32)
    pieces = []
    for offset in range(0, extent, block_size):
        target = places[offset : offset + block_size]
        table = (places[:, None] - target[None, :]) ** 2
        layout = [1] * (values.ndim + 1)
        layout[along] = extent
        layout[along + 1] = block_size
        summed = jnp.expand_dims(values, along + 1) + table.reshape(layout)
        pieces.append(jnp.min(summed, axis=along))
    return jnp.concatenate(pieces, axis=along)


def seed_fields(lowest_cost, occupied, unknown):
    merged_cost = lowest_cost.astype(jnp.float32)
    outside = jnp.where(occupied == 1, merged_cost, merged_cost + penalty)
    inside = jnp.where((occupied == 1) | (unknown == 1), merged_cost + penalty, merged_cost)
    return jnp.stack([outside, inside])


def plain_body(seed_cost, occupied, unknown):
    local_lowest = jnp.min(seed_cost, axis=0)
    merged = lax.pmin(local_lowest, "robot")
    fields = lower_envelope(seed_fields(merged, occupied, unknown), 1)
    half_depth = fields.shape[1] // lax.axis_size("robot")
    own_half = lax.dynamic_slice_in_dim(fields, lax.axis_index("robot") * half_depth, half_depth, 1)
    crossed = lower_envelope(lax.all_to_all(own_half, "xy", split_axis=1, concat_axis=2, tiled=True), 2)
    settled = lower_envelope(lax.all_to_all(crossed, "yz", split_axis=2, concat_axis=3, tiled=True), 3)
    return voxel_size * (jnp.sqrt(settled[0]) - jnp.sqrt(settled[1]))


def encode(field):
    scaled = jnp.log(1.0 + sharpness * field) * (codes / span) + 0.5
    return (jnp.minimum(scaled, codes).astype(jnp.int32) - 32768).astype(jnp.int16)


def decode(code):
    scaled = (code.astype(jnp.int32) + 32768).astype(jnp.float32)
    return (jnp.exp(scaled * (span / codes)) - 1.0) * (1.0 / sharpness)


def depth_kernel(
    cost_ref, occupied_ref, unknown_ref, out_ref, in_ref,
    cost_other, cost_own, occupied_own, unknown_own, gone, come, code, g_ref, h_ref,
    other_sem, own_sem, gone_sem, come_sem, send_sem, recv_sem, keep_sem,
):
    robots, groups = lax.axis_size("robot"), lax.axis_size("xy")
    robot, group = lax.axis_index("robot"), lax.axis_index("xy")
    members = robots * groups
    me = robot * groups + group
    chunks, depth, rows, lanes = gone.shape
    half = chunks * rows
    tile = depth // members
    reach = math.isqrt(int(largest_cost)) + 1

    def place(member):
        return {"robot": member // groups, "xy": lax.rem(member, groups)}

    def span_of(owner, c):
        return pl.ds(pl.multiple_of(owner * half + c * rows, rows), rows)

    def fetch_other(c):
        return pltpu.make_async_copy(cost_ref.at[:, :, span_of(1 - robot, c), :], cost_other.at[c], other_sem.at[c])

    def fetch_own(c):
        return (
            pltpu.make_async_copy(cost_ref.at[:, :, span_of(robot, c), :], cost_own.at[c], own_sem.at[0, c]),
            pltpu.make_async_copy(occupied_ref.at[:, span_of(robot, c), :], occupied_own.at[c], own_sem.at[1, c]),
            pltpu.make_async_copy(unknown_ref.at[:, span_of(robot, c), :], unknown_own.at[c], own_sem.at[2, c]),
        )

    def hand_over(c):
        return pltpu.make_async_remote_copy(
            src_ref=gone.at[c], dst_ref=come.at[c], send_sem=gone_sem.at[c], recv_sem=come_sem.at[c],
            device_id={"robot": 1 - robot}, device_id_type=pl.DeviceIdType.MESH,
        )

    def send(c, step):
        member = lax.rem(me + step, members)
        return pltpu.make_async_remote_copy(
            src_ref=code.at[0, c, pl.ds(member * tile, tile)], dst_ref=out_ref.at[me, :, span_of(0, c), :],
            send_sem=send_sem.at[c, step - 1], recv_sem=recv_sem.at[c, step - 1],
            device_id=place(member), device_id_type=pl.DeviceIdType.MESH,
        )

    def keep(c):
        return (
            pltpu.make_async_copy(code.at[0, c, pl.ds(me * tile, tile)], out_ref.at[me, :, span_of(0, c), :], keep_sem.at[0, c]),
            pltpu.make_async_copy(code.at[1, c], in_ref.at[:, span_of(0, c), :], keep_sem.at[1, c]),
        )

    def over_chunks(do):
        def step(c, _):
            do(c)
            return 0

        lax.fori_loop(0, chunks, step, 0)

    def begin(c):
        fetch_other(c).start()

    over_chunks(begin)

    def begin_own(c):
        for copy in fetch_own(c):
            copy.start()

    over_chunks(begin_own)

    barrier = pltpu.get_barrier_semaphore()
    for step in range(1, members):
        pl.semaphore_signal(barrier, inc=1, device_id=place(lax.rem(me + step, members)), device_id_type=pl.DeviceIdType.MESH)
    pl.semaphore_wait(barrier, members - 1)

    def merge(c):
        fetch_other(c).wait()
        gone[c] = jnp.minimum(cost_other[c, 0], cost_other[c, 1])
        hand_over(c).start()

    over_chunks(merge)

    wall = jnp.full((rows, lanes), far_away, jnp.float32)
    nothing = jnp.zeros((rows, lanes), jnp.float32)
    for field in range(2):
        for pad in range(reach):
            g_ref[field, pad] = wall
            g_ref[field, depth + reach + pad] = wall

    def pass_chunk(c):
        for copy in fetch_own(c):
            copy.wait()
        hand_over(c).wait_recv()

        def seeds(z, carry):
            merged = jnp.minimum(jnp.minimum(cost_own[c, 0, z], cost_own[c, 1, z]), come[c, z]).astype(jnp.float32)
            occupied = occupied_own[c, z] == 1
            blocked = occupied | (unknown_own[c, z] == 1)
            fields = (jnp.where(occupied, merged, merged + penalty), jnp.where(blocked, merged + penalty, merged))
            after = []
            for field, (cost, away) in zip(range(2), carry):
                value = fields[field]
                g_ref[field, z + reach] = value
                seed = value < penalty
                cost = jnp.where(seed, value, cost)
                away = jnp.where(seed, 0.0, away + 1.0)
                h_ref[field, z] = cost + away * away
                after.append((cost, away))
            return tuple(after)

        lax.fori_loop(0, depth, seeds, ((wall, nothing), (wall, nothing)), unroll=4)

        def settle(step, carry):
            z = depth - 1 - step
            after = []
            for field, (cost, away) in zip(range(2), carry):
                value = g_ref[field, z + reach]
                seed = value < penalty
                cost = jnp.where(seed, value, cost)
                away = jnp.where(seed, 0.0, away + 1.0)
                best = jnp.minimum(jnp.minimum(h_ref[field, z], cost + away * away), value)
                for apart in range(1, reach + 1):
                    pair = jnp.minimum(g_ref[field, z + reach - apart], g_ref[field, z + reach + apart])
                    best = jnp.minimum(best, pair + float(apart * apart))
                code[field, c, z] = encode(best)
                after.append((cost, away))
            return tuple(after)

        lax.fori_loop(0, depth, settle, ((wall, nothing), (wall, nothing)), unroll=4)
        for step in range(1, members):
            send(c, step).start()
        for copy in keep(c):
            copy.start()

    over_chunks(pass_chunk)

    def finish(c):
        hand_over(c).wait_send()
        for copy in keep(c):
            copy.wait()
        for step in range(1, members):
            send(c, step).wait()

    over_chunks(finish)


def depth_pass(seed_cost, occupied, unknown, half, members):
    robots, depth, _, lanes = seed_cost.shape
    rows = 16
    chunks = half // rows
    reach = math.isqrt(int(largest_cost)) + 1
    anywhere = pl.BlockSpec(memory_space=pl.ANY)
    copies = pltpu.SemaphoreType.DMA
    return pl.pallas_call(
        depth_kernel,
        out_shape=(
            jax.ShapeDtypeStruct((members, depth // members, half, lanes), jnp.int16),
            jax.ShapeDtypeStruct((depth, half, lanes), jnp.int16),
        ),
        in_specs=[anywhere] * 3,
        out_specs=(anywhere, anywhere),
        scratch_shapes=[
            pltpu.VMEM((chunks, robots, depth, rows, lanes), jnp.bfloat16),
            pltpu.VMEM((chunks, robots, depth, rows, lanes), jnp.bfloat16),
            pltpu.VMEM((chunks, depth, rows, lanes), jnp.int32),
            pltpu.VMEM((chunks, depth, rows, lanes), jnp.int32),
            pltpu.VMEM((chunks, depth, rows, lanes), jnp.bfloat16),
            pltpu.VMEM((chunks, depth, rows, lanes), jnp.bfloat16),
            pltpu.VMEM((2, chunks, depth, rows, lanes), jnp.int16),
            pltpu.VMEM((2, depth + 2 * reach, rows, lanes), jnp.float32),
            pltpu.VMEM((2, depth, rows, lanes), jnp.float32),
            copies((chunks,)),
            copies((3, chunks)),
            copies((chunks,)),
            copies((chunks,)),
            copies((chunks, members - 1)),
            copies((chunks, members - 1)),
            copies((2, chunks)),
        ],
        compiler_params=pltpu.CompilerParams(vmem_limit_bytes=56 * 2**20, collective_id=0, has_side_effects=True),
        name="depth_pass",
    )(seed_cost, occupied, unknown)


def envelope(f_ref, h_ref, low_ref, top_ref, bits_ref, reach_ref, near_ref, list_ref, extent, tile):
    blocks = extent // block
    words = -(-blocks // 32)

    def source(j):
        return pl.ds(pl.multiple_of((margin + j) * tile, tile), tile)

    def target(i):
        return pl.ds(pl.multiple_of(i * tile, tile), tile)

    for pad in range(margin):
        for place in (pad, margin + extent + pad):
            f_ref[place * tile : (place + 1) * tile, :] = jnp.full((tile, 128), far_away, jnp.float32)
    for gap in range(blocks):
        reach = float((gap * block + block - 1) ** 2)
        near = float(max((gap - 1) * block, margin) + 1) ** 2
        for index in {blocks - gap, blocks + gap}:
            reach_ref[index] = jnp.full((tile, 128), reach, jnp.float32)
            near_ref[index] = jnp.full((tile, 128), near, jnp.float32)

    def own(b, _):
        g = [f_ref[source(b * block + k - margin), :] for k in range(block + 2 * margin)]
        low_ref[b] = functools.reduce(jnp.minimum, g[margin : margin + block])
        top = None
        for i in range(block):
            best = g[margin + i]
            for apart in range(1, margin + 1):
                pair = jnp.minimum(g[margin + i - apart], g[margin + i + apart])
                best = jnp.minimum(best, pair + float(apart**2))
            h_ref[target(b * block + i), :] = best
            top = best if top is None else jnp.maximum(top, best)
        top_ref[b] = top
        return 0

    lax.fori_loop(0, blocks, own, 0)

    def bound(group, count):
        for r in range(8):
            b = group * 8 + r
            top = top_ref[b]
            for j in range(blocks):
                top = jnp.minimum(top, low_ref[j] + reach_ref[blocks + b - j])
            for word in range(words):
                bits = jnp.zeros(top.shape, jnp.int32)
                for j in range(word * 32, min(blocks, word * 32 + 32)):
                    value = 1 << (j % 32)
                    value = value - 2**32 if value >= 2**31 else value
                    bits = bits | jnp.where(low_ref[j] + near_ref[blocks + b - j] < top, jnp.int32(value), jnp.int32(0))
                bits_ref[word, pl.ds(r * tile, tile), :] = bits
        for word in range(words):
            joined = functools.reduce(jnp.bitwise_or, [bits_ref[word, pl.ds(k, 8, stride=tile), :] for k in range(tile)])
            shift = 64
            while shift:
                joined = joined | pltpu.roll(joined, shift, 1)
                shift //= 2
            for r in range(8):
                mask = joined[r, 0]
                for first in range(word * 32, min(blocks, word * 32 + 32), 8):
                    some = lax.shift_right_logical(mask, first % 32) & 255

                    def enlist(count, some=some, first=first, b=group * 8 + r):
                        for j in range(8):
                            list_ref[count] = b * 1024 + (first + j)
                            count = count + (lax.shift_right_logical(some, j) & 1)
                        return count

                    count = lax.cond(some != 0, enlist, lambda count: count, count)
        return count

    count = lax.fori_loop(0, blocks // 8, bound, jnp.int32(0))

    def visit(k, _):
        code = list_ref[k]
        b = lax.shift_right_logical(code, 10)
        j = code & 1023
        apart = jnp.full((tile, 128), ((b - j) * block).astype(jnp.float32))
        square = {}
        for step in range(1 - block, block):
            gap = apart + float(step)
            square[step] = gap * gap
        best = [h_ref[target(b * block + i), :] for i in range(block)]
        for step in range(block):
            g = f_ref[source(j * block + step), :]
            best = [jnp.minimum(best[i], g + square[i - step]) for i in range(block)]
        for i in range(block):
            h_ref[target(b * block + i), :] = best[i]
        return 0

    lax.fori_loop(0, count, visit, 0)


def row_kernel(in_ref, out_ref, f_ref, h_ref, *rest, robots):
    sources, tile, part, _ = in_ref.shape
    groups = sources // robots
    extent = sources * part
    targets, _, wide, _ = out_ref.shape

    def load(source, _):
        start = (margin + (lax.rem(source, groups) * robots + source // groups) * part) * tile
        for z in range(tile):
            f_ref[pl.ds(start + z, part, stride=tile), :] = decode(in_ref[source, z])
        return 0

    lax.fori_loop(0, sources, load, 0)
    envelope(f_ref, h_ref, *rest, extent, tile)

    def store(target, _):
        for z in range(tile):
            out_ref[target, z] = encode(h_ref[pl.ds(target * wide * tile + z, wide, stride=tile), :])
        return 0

    lax.fori_loop(0, targets, store, 0)


def column_kernel(in_ref, *refs, has_prior):
    prior_ref, refs = (refs[0], refs[1:]) if has_prior else (None, refs)
    out_ref, f_ref, h_ref, *rest = refs
    sources, tile, _, part = in_ref.shape

    def load(z, _):
        for source in range(sources):
            start = (margin + source * part) * tile
            f_ref[pl.ds(start + z, part, stride=tile), :] = decode(in_ref[source, z]).T
        return 0

    lax.fori_loop(0, tile, load, 0)
    envelope(f_ref, h_ref, *rest, sources * part, tile)

    def store(z, _):
        for source in range(sources):
            lanes = pl.ds(source * part, part)
            root = jnp.sqrt(h_ref[pl.ds(source * part * tile + z, part, stride=tile), :]).T
            if has_prior:
                root = voxel_size * (prior_ref[z, :, lanes] - root)
            out_ref[z, :, lanes] = root
        return 0

    lax.fori_loop(0, tile, store, 0)


def scratch(extent, tile):
    blocks = extent // block
    words = -(-blocks // 32)
    return [
        pltpu.VMEM(((extent + 2 * margin) * tile, 128), jnp.float32),
        pltpu.VMEM((extent * tile, 128), jnp.float32),
        pltpu.VMEM((blocks, tile, 128), jnp.float32),
        pltpu.VMEM((blocks, tile, 128), jnp.float32),
        pltpu.VMEM((words, 8 * tile, 128), jnp.int32),
        pltpu.VMEM((2 * blocks, tile, 128), jnp.float32),
        pltpu.VMEM((2 * blocks, tile, 128), jnp.float32),
        pltpu.SMEM((blocks * blocks + 1,), jnp.int32),
    ]


def whole_call(kernel, shape, extent, tile, name, *operands):
    vmem = pl.BlockSpec(memory_space=pltpu.VMEM)
    return pl.pallas_call(
        kernel,
        out_shape=shape,
        in_specs=[vmem] * len(operands),
        out_specs=vmem,
        scratch_shapes=scratch(extent, tile),
        compiler_params=pltpu.CompilerParams(vmem_limit_bytes=56 * 2**20),
        name=name,
    )(*operands)


def row_pass(received, robots, targets, name):
    sources, tile, part, lanes = received.shape
    extent = sources * part
    shape = jax.ShapeDtypeStruct((targets, tile, extent // targets, lanes), jnp.int16)
    return whole_call(functools.partial(row_kernel, robots=robots), shape, extent, tile, name, received)


def column_pass(received, name, *prior):
    sources, tile, rows, part = received.shape
    shape = jax.ShapeDtypeStruct((tile, rows, sources * part), jnp.float32)
    return whole_call(functools.partial(column_kernel, has_prior=bool(prior)), shape, sources * part, tile, name, received, *prior)


def fast_body(seed_cost, occupied, unknown):
    robots = lax.axis_size("robot")
    groups = lax.axis_size("xy")
    strips = lax.axis_size("yz")
    depth, rows, lanes = occupied.shape
    half = rows // robots
    tile = depth // (robots * groups)
    members = robots * groups
    out_received, in_codes = depth_pass(seed_cost, occupied, unknown, half, members)
    in_received = lax.all_to_all(
        in_codes.reshape(members, tile, half, lanes), ("robot", "xy"), split_axis=0, concat_axis=0, tiled=True
    )
    settled = []
    for received, label in ((out_received, "out"), (in_received, "in")):
        crossed = row_pass(received, robots, strips, "row_pass_" + label)
        received = lax.all_to_all(crossed, "yz", split_axis=0, concat_axis=0, tiled=True)
        settled = [column_pass(received, "column_pass_" + label, *settled)]
    return settled[0]


def body(seed_cost, occupied, unknown):
    robots, groups, strips = (lax.axis_size(name) for name in ("robot", "xy", "yz"))
    depth, rows, lanes = occupied.shape
    fits = (
        robots == 2
        and seed_cost.shape[0] == 2
        and lanes == 128
        and rows % (16 * robots) == 0
        and depth == 8 * robots * groups
        and rows * groups == 128 * strips
        and rows * groups % (8 * block) == 0
        and (depth - 1) ** 2 + largest_cost < penalty
    )
    return (fast_body if fits else plain_body)(seed_cost, occupied, unknown)


def solution(mesh):
    in_specs = (P("robot", None, "xy", "yz"), P(None, "xy", "yz"), P(None, "xy", "yz"))
    out_specs = P(("robot", "xy"), "yz", None)
    return jax.shard_map(body, mesh=mesh, in_specs=in_specs, out_specs=out_specs, check_vma=False)
```
